32 devices in a mesh: island: 2 (over x), fsdp: 16 (over z, y, core).
Axes of the slice: x: 2, y: 2, z: 4, core: 2. Of those that a mesh axis runs over, the one named last changes fastest.
Arguments:
- partial_grads: bfloat16 [2, 16, 48, 28672], P('island', 'fsdp'), may hold values from -4 to 4, as said below
- inner_weights: bfloat16 [2, 48, 28672], P('island'), may hold values from -6 to 6
- outer_weights: float32 [48, 28672], P(None, 'fsdp'), may hold values from -6 to 6
- momentum: float32 [48, 28672], P(None, 'fsdp'), may hold values from -6 to 6
- round_draws: int32 [2, 48, 28672], P('island', None, 'fsdp'), may hold values from 0 to 255
- scale_exps: int32 [2, 48, 224], P('island', None, 'fsdp'), may hold values from -3 to 0
Outputs:
- new_outer: float32 [48, 28672], P(None, 'fsdp')
- new_momentum: float32 [48, 28672], P(None, 'fsdp')
- mixed_inner: bfloat16 [2, 48, 28672], P('island')
The draws below stay inside these ranges and needn't reach their ends.
Inputs may be any that keep to these rules, and one draw needn't show every extreme that they name: `partial_grads`: every nonzero entry has magnitude 1/64 or more.
All inputs are finite; a program needn't handle non-finite values.
Results may differ from the reference program's by a relative error of at most 0.0054.
Values may be sent and summed in bfloat16 or wider, within the bound.
A program may use at most 64 MiB of HBM per device.

```python
import jax
import jax.numpy as jnp
from jax import lax

FF = 28672
ROWS = 48
BLOCK = 128
ISLANDS = 2
SHARDS = 16


def draw_partial_grads(key, part):
    key_base = jax.random.fold_in(key, 0)
    values = jnp.clip(jax.random.normal(key_base, (ISLANDS, SHARDS, ROWS, FF), jnp.float32), -4.0, 4.0)
    values = jnp.where(jnp.abs(values) < 0.015625, 0.0, values)
    return values.astype(jnp.bfloat16)


def set_ends(array, own_key, least, high):
    place = [jax.random.randint(jax.random.fold_in(own_key, axis), (), 0, length) for axis, length in enumerate(array.shape)]
    main_axis = array.shape.index(max(array.shape))
    beside = place[:main_axis] + [(place[main_axis] + 1) % array.shape[main_axis]] + place[main_axis + 1:]
    return array.at[tuple(place)].set(least).at[tuple(beside)].set(high)


def level_of(key, dims, shards, smallest, high):
    def one(dim, parts):
        steps = jax.random.uniform(jax.random.fold_in(jax.random.fold_in(key, 6), dim), (parts,), jnp.float32, smallest / len(shards), high / len(shards))
        return jnp.repeat(jnp.exp(steps), dims[dim] // parts).reshape((-1,) + (1,) * (len(dims) - dim - 1))

    loudness = one(*shards[0])
    for cut in shards[1:]:
        loudness = loudness * one(*cut)
    return loudness


def gaussian(stream_key, extent, scale, most, cuts=(), kind=jnp.bfloat16):
    entries = scale * jax.random.normal(stream_key, extent, jnp.float32)
    if cuts:
        entries = entries * level_of(stream_key, extent, cuts, -0.22, 0.18)
    return jnp.clip(entries, -most, most).astype(kind)


def setup_inputs(seed: int = 0) -> dict:
    keys = jax.random.split(jax.random.key(seed), 7)
    partial_grads = draw_partial_grads(jax.random.fold_in(keys[6], 71), 0)
    inner_weights = gaussian(keys[1], (ISLANDS, ROWS, FF), 1.0, 6.0, ((0, 2),))
    outer_weights = gaussian(keys[2], (ROWS, FF), 1.0, 6.0, ((1, 16),), jnp.float32)
    momentum = gaussian(keys[3], (ROWS, FF), 1.0, 6.0, ((1, 16),), jnp.float32)
    round_draws = set_ends(jax.random.randint(keys[4], (ISLANDS, ROWS, FF), 0, 256), jax.random.fold_in(keys[4], 1), 0, 255).astype(jnp.int32)
    scale_exps = set_ends(jax.random.randint(keys[5], (ISLANDS, ROWS, FF // BLOCK), -3, 1), jax.random.fold_in(keys[5], 1), -3, 0).astype(jnp.int32)
    return {"partial_grads": partial_grads, "inner_weights": inner_weights, "outer_weights": outer_weights, "momentum": momentum, "round_draws": round_draws, "scale_exps": scale_exps}


OUTER_RATE = 0.7
MOMENTUM_COEF = 0.9
MIX_WEIGHT = 0.5


def quantize(pseudo, round_draws, exponents):
    height = pseudo.shape[0]
    blocks = exponents.shape[-1]
    powers = jnp.left_shift(jnp.ones_like(exponents), exponents + 8).astype(jnp.float32) / 256.0
    scaled = pseudo.reshape(height, blocks, -1) / powers[..., None]
    dither = round_draws.reshape(height, blocks, -1).astype(jnp.float32) / 256.0
    levels = jnp.clip(jnp.floor(scaled + dither), -127.0, 127.0)
    return (levels * powers[..., None]).reshape(pseudo.shape)


def one_island(island_args):
    grad_terms, round_draws, exponents = island_args
    pseudo = jnp.sum(grad_terms.astype(jnp.float32), axis=0)
    return quantize(pseudo, round_draws, exponents)


def reference(partial_grads, inner_weights, outer_weights, momentum, round_draws, scale_exps):
    dequant = lax.map(one_island, (partial_grads, round_draws, scale_exps))
    average = jnp.sum(dequant, axis=0) / ISLANDS
    new_momentum = MOMENTUM_COEF * momentum + average
    new_outer = outer_weights - OUTER_RATE * (average + MOMENTUM_COEF * new_momentum)
    outer_half = lax.optimization_barrier(new_outer.astype(jnp.bfloat16))
    mixed_inner = (MIX_WEIGHT * inner_weights.astype(jnp.float32)
                   + (1.0 - MIX_WEIGHT) * outer_half.astype(jnp.float32)[None]).astype(jnp.bfloat16)
    return new_outer, new_momentum, mixed_inner
```

```python
import functools

import jax
import jax.numpy as jnp
from jax import lax
from jax.experimental import pallas as pl
from jax.experimental.pallas import tpu as pltpu
from jax.sharding import PartitionSpec as P

OUTER_RATE = 0.7
MOMENTUM_COEF = 0.9
MIX_WEIGHT = 0.5

MESH = pl.DeviceIdType.MESH
CHUNK = 16
LINE = 4
UNIT = 8192.0
LOW = 4


def remote(src, dst, send, recv, device):
    return pltpu.make_async_remote_copy(
        src_ref=src, dst_ref=dst, send_sem=send, recv_sem=recv,
        device_id=device, device_id_type=MESH,
    )


def kernel(A, B, I, W, R, grads, inner, outer, moment, draws, exps,
           new_outer, new_moment, mixed,
           mine, peer, sb, rb, sa, ra, acc, own_q, sx, rx, gat, blend,
           l1, s1, r1, s2, r2, s3, r3, s4, r4, s5, r5, s6, r6, s7, r7, inner_sem, out_sem):
    AB = A * B
    L = 128 * (-(-(W // 128) // 4))
    isl = lax.axis_index("island")
    f = lax.axis_index("fsdp")
    c = lax.rem(f, 2)
    ab = f // 2
    b = lax.rem(ab, B)
    a = ab // B
    core_dev = (isl, 2 * ab + 1 - c)

    def b_dev(k):
        return (isl, (a * B + lax.rem(b + k, B)) * 2 + c)

    def a_dev(k):
        return (isl, (lax.rem(a + k, A) * B + b) * 2 + c)

    def i_dev(k):
        return (lax.rem(isl + k, I), f)

    partners = ([core_dev] + [b_dev(k) for k in range(1, B)] + [a_dev(k) for k in range(1, A)]
                + [i_dev(k) for k in range(1, I)])

    def columns(block):
        return pl.ds(pl.multiple_of(block * W, 128), W)

    def rows(r):
        return pl.ds(r * CHUNK, CHUNK)

    inner_copy = pltpu.make_async_copy(inner, blend, inner_sem.at[0])
    inner_copy.start()
    for r in range(R):
        for j in range(AB):
            pltpu.make_async_copy(grads.at[rows(r), columns(2 * j + c)], mine.at[r, j], l1.at[r]).start()

    barrier = pltpu.get_barrier_semaphore()
    for device in partners:
        pl.semaphore_signal(barrier, inc=1, device_id=device, device_id_type=MESH)
    pl.semaphore_wait(barrier, len(partners))

    sends = []

    def begin(copy):
        copy.start()
        sends.append(copy)

    for r in range(R):
        for j in range(AB):
            remote(grads.at[rows(r), columns(2 * j + 1 - c)], peer.at[r, j], s1.at[r], r1.at[r], core_dev).start()

    def pair_sum(r, block):
        total = mine[r, block].astype(jnp.float32) + peer[r, block].astype(jnp.float32)
        return (total * UNIT).astype(jnp.int32)

    def stage1(r):
        pltpu.make_async_copy(mine.at[r], mine.at[r], l1.at[r]).wait()
        remote(peer.at[r], peer.at[r], s1.at[r], r1.at[r], core_dev).wait_recv()
        for k in range(1, B):
            target = lax.rem(b + k, B)
            low = None
            for j in range(A):
                s = pair_sum(r, j * B + target)
                sb[r, k - 1, j] = lax.shift_right_arithmetic(s, LOW).astype(jnp.int16)
                part = jnp.left_shift(jnp.bitwise_and(s, 15), LOW * j)
                low = part if low is None else low + part
            sb[r, k - 1, A] = low.astype(jnp.int16)
            begin(remote(sb.at[r, k - 1], rb.at[r, k - 1], s2.at[r, k - 1], r2.at[r, k - 1], b_dev(k)))

    def stage2(r):
        for k in range(1, B):
            remote(sb.at[r, k - 1], rb.at[r, k - 1], s2.at[r, k - 1], r2.at[r, k - 1], b_dev(k)).wait_recv()

        def column_sum(j):
            s = pair_sum(r, j * B + b)
            for k in range(1, B):
                high = jnp.left_shift(rb[r, k - 1, j].astype(jnp.int32), LOW)
                low = lax.shift_right_arithmetic(
                    rb[r, k - 1, A].astype(jnp.int32), jnp.full((CHUNK, W), LOW * j, jnp.int32))
                s = s + high + jnp.bitwise_and(low, 15)
            return s

        for k in range(1, A):
            s = column_sum(lax.rem(a + k, A))
            sa[r, k - 1, :, :W] = lax.shift_right_arithmetic(s, LOW).astype(jnp.int16)
            low = jnp.bitwise_and(s, 15)
            low = jnp.concatenate([low, jnp.zeros((CHUNK, 4 * L - W), jnp.int32)], axis=1) if 4 * L > W else low
            packed = low[:, :L]
            for q in range(1, 4):
                packed = packed + jnp.left_shift(low[:, q * L:(q + 1) * L], LOW * q)
            sa[r, k - 1, :, W:] = packed.astype(jnp.int16)
            begin(remote(sa.at[r, k - 1], ra.at[r, k - 1], s3.at[r, k - 1], r3.at[r, k - 1], a_dev(k)))
        acc[r] = column_sum(a)

    def powers(r, sign):
        e = exps[r * CHUNK:(r + 1) * CHUNK, :]
        p = jnp.left_shift(jnp.ones_like(e), 8 + sign * e).astype(jnp.float32) / 256.0
        return jnp.concatenate(
            [jnp.broadcast_to(p[:, t:t + 1], (CHUNK, 128)) for t in range(W // 128)], axis=1)

    def stage3(r):
        total = acc[r]
        for k in range(1, A):
            remote(sa.at[r, k - 1], ra.at[r, k - 1], s3.at[r, k - 1], r3.at[r, k - 1], a_dev(k)).wait_recv()
            high = jnp.left_shift(ra[r, k - 1, :, :W].astype(jnp.int32), LOW)
            packed = ra[r, k - 1, :, W:].astype(jnp.int32)
            low = jnp.concatenate(
                [jnp.bitwise_and(lax.shift_right_arithmetic(packed, jnp.full_like(packed, LOW * q)), 15)
                 for q in range(4)], axis=1)[:, :W]
            total = total + high + low
        pseudo = total.astype(jnp.float32) * (1.0 / UNIT)
        dither = draws[r * CHUNK:(r + 1) * CHUNK, :].astype(jnp.float32) * (1.0 / 256.0)
        levels = jnp.clip(jnp.floor(pseudo * powers(r, -1) + dither), -127.0, 127.0)
        dequant = levels * powers(r, 1)
        own_q[r] = dequant
        sx[r] = dequant.astype(jnp.bfloat16)
        for k in range(1, I):
            begin(remote(sx.at[r], rx.at[r, k - 1], s4.at[r, k - 1], r4.at[r, k - 1], i_dev(k)))

    def stage4(r):
        total = own_q[r]
        for k in range(1, I):
            remote(sx.at[r], rx.at[r, k - 1], s4.at[r, k - 1], r4.at[r, k - 1], i_dev(k)).wait_recv()
            total = total + rx[r, k - 1].astype(jnp.float32)
        average = total / I
        at = slice(r * CHUNK, (r + 1) * CHUNK)
        moment_next = MOMENTUM_COEF * moment[at, :] + average
        outer_next = outer[at, :] - OUTER_RATE * (average + MOMENTUM_COEF * moment_next)
        new_moment[at, :] = moment_next
        new_outer[at, :] = outer_next
        gat[r, c, b, a] = outer_next.astype(jnp.bfloat16)
        for k in range(1, A):
            begin(remote(gat.at[r, c, b, a], gat.at[r, c, b, a], s5.at[r, k - 1], r5.at[r, k - 1], a_dev(k)))

    def stage5(r):
        for k in range(1, A):
            came = gat.at[r, c, b, lax.rem(a + A - k, A)]
            remote(came, came, s5.at[r, k - 1], r5.at[r, k - 1], a_dev(k)).wait_recv()
        for k in range(1, B):
            begin(remote(gat.at[r, c, b], gat.at[r, c, b], s6.at[r, k - 1], r6.at[r, k - 1], b_dev(k)))

    def stage6(r):
        for k in range(1, B):
            came = gat.at[r, c, lax.rem(b + B - k, B)]
            remote(came, came, s6.at[r, k - 1], r6.at[r, k - 1], b_dev(k)).wait_recv()
        begin(remote(gat.at[r, c], gat.at[r, c], s7.at[r], r7.at[r], core_dev))

    def stage7(r):
        came = gat.at[r, 1 - c]
        remote(came, came, s7.at[r], r7.at[r], core_dev).wait_recv()
        if r == 0:
            inner_copy.wait()
        at = slice(r * CHUNK, (r + 1) * CHUNK)
        for core in range(2):
            for y in range(B):
                for z in range(A):
                    block = (z * B + y) * 2 + core
                    span = slice(block * W, (block + 1) * W)
                    value = MIX_WEIGHT * blend[at, span].astype(jnp.float32)
                    value = value + (1.0 - MIX_WEIGHT) * gat[r, core, y, z].astype(jnp.float32)
                    blend[at, span] = value.astype(jnp.bfloat16)
        pltpu.make_async_copy(blend.at[rows(r)], mixed.at[rows(r)], out_sem.at[r]).start()

    stages = [stage1, stage2, stage3, stage4, stage5, stage6, stage7]
    for t in range(R + len(stages) - 1):
        for index in range(len(stages)):
            r = t - index
            if 0 <= r < R:
                stages[index](r)

    for copy in sends:
        copy.wait_send()
    for r in range(R):
        remote(peer.at[r], peer.at[r], s1.at[r], r1.at[r], core_dev).wait_send()
        pltpu.make_async_copy(blend.at[rows(r)], mixed.at[rows(r)], out_sem.at[r]).wait()


def solution(mesh):
    I, n = mesh.shape["island"], mesh.shape["fsdp"]
    A = LINE
    B = n // (2 * A)

    def on_device(grads, inner, outer, moment, draws, exps):
        height, W = outer.shape
        R = height // CHUNK
        L = 128 * (-(-(W // 128) // 4))
        any_spec = pl.BlockSpec(memory_space=pl.ANY)
        vmem = pl.BlockSpec(memory_space=pltpu.VMEM)
        bf16, i16, f32, i32 = jnp.bfloat16, jnp.int16, jnp.float32, jnp.int32
        dma = pltpu.SemaphoreType.DMA
        bm, im = max(B - 1, 1), max(I - 1, 1)
        out = pl.pallas_call(
            functools.partial(kernel, A, B, I, W, R),
            out_shape=(
                jax.ShapeDtypeStruct(outer.shape, f32),
                jax.ShapeDtypeStruct(moment.shape, f32),
                jax.ShapeDtypeStruct(inner.shape[1:], bf16),
            ),
            in_specs=[any_spec, any_spec, vmem, vmem, vmem, vmem],
            out_specs=(vmem, vmem, any_spec),
            scratch_shapes=[
                pltpu.VMEM((R, A * B, CHUNK, W), bf16),
                pltpu.VMEM((R, A * B, CHUNK, W), bf16),
                pltpu.VMEM((R, bm, A + 1, CHUNK, W), i16),
                pltpu.VMEM((R, bm, A + 1, CHUNK, W), i16),
                pltpu.VMEM((R, A - 1, CHUNK, W + L), i16),
                pltpu.VMEM((R, A - 1, CHUNK, W + L), i16),
                pltpu.VMEM((R, CHUNK, W), i32),
                pltpu.VMEM((R, CHUNK, W), f32),
                pltpu.VMEM((R, CHUNK, W), bf16),
                pltpu.VMEM((R, im, CHUNK, W), bf16),
                pltpu.VMEM((R, 2, B, A, CHUNK, W), bf16),
                pltpu.VMEM(inner.shape[1:], bf16),
                dma((R,)), dma((R,)), dma((R,)),
                dma((R, bm)), dma((R, bm)),
                dma((R, A - 1)), dma((R, A - 1)),
                dma((R, im)), dma((R, im)),
                dma((R, A - 1)), dma((R, A - 1)),
                dma((R, bm)), dma((R, bm)),
                dma((R,)), dma((R,)),
                dma((1,)), dma((R,)),
            ],
            compiler_params=pltpu.CompilerParams(
                collective_id=0, has_side_effects=True, vmem_limit_bytes=48 * 1024 * 1024,
            ),
        )(grads[0, 0], inner[0], outer, moment, draws[0], exps[0])
        return out[0], out[1], out[2][None]

    in_specs = (
        P("island", "fsdp", None, None),
        P("island", None, None),
        P(None, "fsdp"),
        P(None, "fsdp"),
        P("island", None, "fsdp"),
        P("island", None, "fsdp"),
    )
    out_specs = (P(None, "fsdp"), P(None, "fsdp"), P("island", None, None))
    return jax.shard_map(
        on_device, mesh=mesh, in_specs=in_specs, out_specs=out_specs, check_vma=False
    )
```

```python
import functools

import jax
import jax.numpy as jnp
from jax import lax
from jax.experimental import pallas as pl
from jax.experimental.pallas import tpu as pltpu
from jax.sharding import PartitionSpec as P

OUTER_RATE = 0.7
MOMENTUM_COEF = 0.9
MIX_WEIGHT = 0.5

MESH = pl.DeviceIdType.MESH
CHUNK = 16
LINE = 4
UNIT = 8192.0
PAIR_LOW = 2


def remote(src, dst, send, recv, device):
    return pltpu.make_async_remote_copy(
        src_ref=src, dst_ref=dst, send_sem=send, recv_sem=recv,
        device_id=device, device_id_type=MESH,
    )


def tiles_up(width, parts):
    return 128 * (-(-(width // 128) // parts))


def shift_right(value, amount):
    return lax.shift_right_arithmetic(value, jnp.full(value.shape, amount, jnp.int32))


def pack_low(value, bits, first, L):
    low = jnp.bitwise_and(value, 2 ** bits - 1)
    width = value.shape[1]
    packed = None
    for q in range(-(-width // L)):
        piece = low[:, q * L:(q + 1) * L]
        if piece.shape[1] < L:
            piece = jnp.concatenate([piece, jnp.zeros((value.shape[0], L - piece.shape[1]), jnp.int32)], axis=1)
        piece = jnp.left_shift(piece, bits * (first + q))
        packed = piece if packed is None else packed + piece
    return packed


def unpack(high, packed, bits, first, L):
    width = high.shape[1]
    low = [jnp.bitwise_and(shift_right(packed, bits * (first + q)), 2 ** bits - 1)
           for q in range(-(-width // L))]
    low = jnp.concatenate(low, axis=1)[:, :width]
    return jnp.left_shift(high.astype(jnp.int32), bits) + low


def kernel(A, B, I, W, R, grads, inner, outer_hbm, moment_hbm, draws_hbm, exps,
           new_outer, new_moment, mixed,
           mine, peer, sb, rb, sa, ra, acc, own_q, sx, rx, gat, blend, outer, moment, draws,
           l1, s1, r1, s2, r2, s3, r3, s4, r4, s5, r5, s6, r6, s7, r7, s8, r8, load_sem):
    AB = A * B
    PL = tiles_up(W, 2)
    ZB = (2 * B).bit_length()
    ZL = tiles_up(W, 16 // ZB)
    H = tiles_up(W, 2)
    isl = lax.axis_index("island")
    f = lax.axis_index("fsdp")
    h = lax.rem(isl, 2)
    c = lax.rem(f, 2)
    ab = f // 2
    b = lax.rem(ab, B)
    a = ab // B
    core_dev = (isl, 2 * ab + 1 - c)
    twin_dev = (isl + 1 - 2 * h, f)

    def b_dev(k):
        return (isl, (a * B + lax.rem(b + k, B)) * 2 + c)

    def a_dev(k):
        return (isl, (lax.rem(a + k, A) * B + b) * 2 + c)

    def i_dev(k):
        return (lax.rem(isl + k, I), f)

    partners = ([core_dev] + [b_dev(k) for k in range(1, B)] + [a_dev(k) for k in range(1, A)]
                + [i_dev(k) for k in range(1, I)])

    def columns(block):
        return pl.ds(pl.multiple_of(block * W, 128), W)

    def rows(r):
        return pl.ds(r * CHUNK, CHUNK)

    for r in range(R):
        for j in range(AB):
            pltpu.make_async_copy(grads.at[rows(r), columns(2 * j + c)], mine.at[r, j], l1.at[r]).start()

    barrier = pltpu.get_barrier_semaphore()
    for device in partners:
        pl.semaphore_signal(barrier, inc=1, device_id=device, device_id_type=MESH)
    pl.semaphore_wait(barrier, len(partners))

    sends = []

    def begin(copy):
        copy.start()
        sends.append(copy)

    for r in range(R):
        for j in range(AB):
            remote(grads.at[rows(r), columns(2 * j + 1 - c)], peer.at[r, j], s1.at[r], r1.at[r], core_dev).start()

    loads = [pltpu.make_async_copy(src, dst, load_sem.at[q]) for q, (src, dst) in enumerate(
        ((draws_hbm, draws), (outer_hbm, outer), (moment_hbm, moment), (inner, blend)))]
    for load in loads:
        load.start()

    def pair_sum(r, block):
        total = mine[r, block].astype(jnp.float32) + peer[r, block].astype(jnp.float32)
        return (total * UNIT).astype(jnp.int32)

    def stage1(r):
        pltpu.make_async_copy(mine.at[r], mine.at[r], l1.at[r]).wait()
        remote(peer.at[r], peer.at[r], s1.at[r], r1.at[r], core_dev).wait_recv()
        for k in range(1, B):
            target = lax.rem(b + k, B)
            low = None
            for j in range(A):
                s = pair_sum(r, j * B + target)
                sb[r, k - 1, :, j * W:(j + 1) * W] = shift_right(s, PAIR_LOW).astype(jnp.int16)
                part = pack_low(s, PAIR_LOW, 2 * j, PL)
                low = part if low is None else low + part
            sb[r, k - 1, :, A * W:] = low.astype(jnp.int16)
            begin(remote(sb.at[r, k - 1], rb.at[r, k - 1], s2.at[r, k - 1], r2.at[r, k - 1], b_dev(k)))

    def stage2(r):
        for k in range(1, B):
            remote(sb.at[r, k - 1], rb.at[r, k - 1], s2.at[r, k - 1], r2.at[r, k - 1], b_dev(k)).wait_recv()

        def column_sum(j):
            s = pair_sum(r, j * B + b)
            for k in range(1, B):
                s = s + unpack(rb[r, k - 1, :, columns(j)], rb[r, k - 1, :, A * W:].astype(jnp.int32),
                               PAIR_LOW, 2 * j, PL)
            return s

        for k in range(1, A):
            s = column_sum(lax.rem(a + k, A))
            sa[r, k - 1, :, :W] = shift_right(s, ZB).astype(jnp.int16)
            sa[r, k - 1, :, W:] = pack_low(s, ZB, 0, ZL).astype(jnp.int16)
            begin(remote(sa.at[r, k - 1], ra.at[r, k - 1], s3.at[r, k - 1], r3.at[r, k - 1], a_dev(k)))
        acc[r] = column_sum(a)

    def powers(r, sign):
        e = exps[r * CHUNK:(r + 1) * CHUNK, :]
        p = jnp.left_shift(jnp.ones_like(e), 8 + sign * e).astype(jnp.float32) / 256.0
        return jnp.concatenate(
            [jnp.broadcast_to(p[:, t:t + 1], (CHUNK, 128)) for t in range(W // 128)], axis=1)

    def stage3(r):
        if r == 0:
            loads[0].wait()
        total = acc[r]
        for k in range(1, A):
            remote(sa.at[r, k - 1], ra.at[r, k - 1], s3.at[r, k - 1], r3.at[r, k - 1], a_dev(k)).wait_recv()
            total = total + unpack(ra[r, k - 1, :, :W], ra[r, k - 1, :, W:].astype(jnp.int32), ZB, 0, ZL)
        pseudo = total.astype(jnp.float32) * (1.0 / UNIT)
        dither = draws[r * CHUNK:(r + 1) * CHUNK, :].astype(jnp.float32) * (1.0 / 256.0)
        levels = jnp.clip(jnp.floor(pseudo * powers(r, -1) + dither), -127.0, 127.0)
        dequant = levels * powers(r, 1)
        own_q[r] = dequant
        sx[r] = dequant.astype(jnp.bfloat16)
        for k in range(1, I):
            begin(remote(sx.at[r], rx.at[r, k - 1], s4.at[r, k - 1], r4.at[r, k - 1], i_dev(k)))

    def stage4(r):
        if r == 0:
            loads[1].wait()
            loads[2].wait()
        total = own_q[r]
        for k in range(1, I):
            remote(sx.at[r], rx.at[r, k - 1], s4.at[r, k - 1], r4.at[r, k - 1], i_dev(k)).wait_recv()
            total = total + rx[r, k - 1].astype(jnp.float32)
        average = total / I
        at = slice(r * CHUNK, (r + 1) * CHUNK)
        moment_next = MOMENTUM_COEF * moment[at, :] + average
        outer_next = outer[at, :] - OUTER_RATE * (average + MOMENTUM_COEF * moment_next)
        new_moment[at, :] = moment_next
        new_outer[at, :] = outer_next
        gat[r, h, c, b, a] = jnp.where(h == 0, outer_next[:, :H], outer_next[:, W - H:]).astype(jnp.bfloat16)
        for k in range(1, A):
            own = gat.at[r, h, c, b, a]
            begin(remote(own, own, s5.at[r, k - 1], r5.at[r, k - 1], a_dev(k)))

    def to_twin(r, k):
        part = gat.at[r, h, c, lax.rem(b + B - k, B)]
        return remote(part, part, s7.at[r, k], r7.at[r, k], twin_dev)

    def to_core(r, other, k):
        part = gat.at[r, 1 - h if other else h, c, lax.rem(b + B - k, B)]
        return remote(part, part, s8.at[r, other, k], r8.at[r, other, k], core_dev)

    def stage5(r):
        for k in range(1, A):
            came = gat.at[r, h, c, b, lax.rem(a + A - k, A)]
            remote(came, came, s5.at[r, k - 1], r5.at[r, k - 1], a_dev(k)).wait_recv()
        line = gat.at[r, h, c, b]
        for k in range(1, B):
            begin(remote(line, line, s6.at[r, k - 1], r6.at[r, k - 1], b_dev(k)))
        begin(to_twin(r, 0))
        begin(to_core(r, 0, 0))

    def stage6(r):
        for k in range(1, B):
            came = gat.at[r, h, c, lax.rem(b + B - k, B)]
            remote(came, came, s6.at[r, k - 1], r6.at[r, k - 1], b_dev(k)).wait_recv()
            begin(to_twin(r, k))
            begin(to_core(r, 0, k))

    def mix(r, core):
        at = slice(r * CHUNK, (r + 1) * CHUNK)
        for half in range(2):
            skip = half * (2 * H - W)
            for y in range(B):
                for z in range(A):
                    begin_at = ((z * B + y) * 2 + core) * W + half * H
                    span = pl.ds(pl.multiple_of(begin_at, 128), H - skip)
                    value = MIX_WEIGHT * blend[at, span].astype(jnp.float32)
                    segment = gat[r, half, core, y, z, :, skip:].astype(jnp.float32)
                    mixed[at, span] = (value + (1.0 - MIX_WEIGHT) * segment).astype(jnp.bfloat16)

    def stage7(r):
        for k in range(B):
            came = gat.at[r, 1 - h, c, lax.rem(b + B - k, B)]
            remote(came, came, s7.at[r, k], r7.at[r, k], twin_dev).wait_recv()
            begin(to_core(r, 1, k))
        if r == 0:
            loads[3].wait()
        mix(r, c)

    def stage8(r):
        for other in range(2):
            for k in range(B):
                came = gat.at[r, 1 - h if other else h, 1 - c, lax.rem(b + B - k, B)]
                remote(came, came, s8.at[r, other, k], r8.at[r, other, k], core_dev).wait_recv()
        mix(r, 1 - c)

    stages = [stage1, stage2, stage3, stage4, stage5, stage6, stage7, stage8]
    for t in range(R + len(stages) - 1):
        for index in range(len(stages)):
            r = t - index
            if 0 <= r < R:
                stages[index](r)

    for copy in sends:
        copy.wait_send()
    for r in range(R):
        remote(peer.at[r], peer.at[r], s1.at[r], r1.at[r], core_dev).wait_send()


def solution(mesh):
    I, n = mesh.shape["island"], mesh.shape["fsdp"]
    A = LINE
    B = n // (2 * A)

    def on_device(grads, inner, outer, moment, draws, exps):
        height, W = outer.shape
        R = height // CHUNK
        PL, H = tiles_up(W, 2), tiles_up(W, 2)
        ZL = tiles_up(W, 16 // (2 * B).bit_length())
        any_spec = pl.BlockSpec(memory_space=pl.ANY)
        vmem = pl.BlockSpec(memory_space=pltpu.VMEM)
        bf16, i16, f32, i32 = jnp.bfloat16, jnp.int16, jnp.float32, jnp.int32
        dma = pltpu.SemaphoreType.DMA
        bm, im = max(B - 1, 1), max(I - 1, 1)
        out = pl.pallas_call(
            functools.partial(kernel, A, B, I, W, R),
            out_shape=(
                jax.ShapeDtypeStruct(outer.shape, f32),
                jax.ShapeDtypeStruct(moment.shape, f32),
                jax.ShapeDtypeStruct(inner.shape[1:], bf16),
            ),
            in_specs=[any_spec, any_spec, any_spec, any_spec, any_spec, vmem],
            out_specs=(vmem, vmem, vmem),
            scratch_shapes=[
                pltpu.VMEM((R, A * B, CHUNK, W), bf16),
                pltpu.VMEM((R, A * B, CHUNK, W), bf16),
                pltpu.VMEM((R, bm, CHUNK, A * W + PL), i16),
                pltpu.VMEM((R, bm, CHUNK, A * W + PL), i16),
                pltpu.VMEM((R, A - 1, CHUNK, W + ZL), i16),
                pltpu.VMEM((R, A - 1, CHUNK, W + ZL), i16),
                pltpu.VMEM((R, CHUNK, W), i32),
                pltpu.VMEM((R, CHUNK, W), f32),
                pltpu.VMEM((R, CHUNK, W), bf16),
                pltpu.VMEM((R, im, CHUNK, W), bf16),
                pltpu.VMEM((R, 2, 2, B, A, CHUNK, H), bf16),
                pltpu.VMEM(inner.shape[1:], bf16),
                pltpu.VMEM(outer.shape, f32),
                pltpu.VMEM(outer.shape, f32),
                pltpu.VMEM(outer.shape, i32),
                dma((R,)), dma((R,)), dma((R,)),
                dma((R, bm)), dma((R, bm)),
                dma((R, A - 1)), dma((R, A - 1)),
                dma((R, im)), dma((R, im)),
                dma((R, A - 1)), dma((R, A - 1)),
                dma((R, bm)), dma((R, bm)),
                dma((R, B)), dma((R, B)),
                dma((R, 2, B)), dma((R, 2, B)),
                dma((4,)),
            ],
            compiler_params=pltpu.CompilerParams(
                collective_id=0, has_side_effects=True, vmem_limit_bytes=48 * 1024 * 1024,
            ),
        )(grads[0, 0], inner[0], outer, moment, draws[0], exps[0])
        return out[0], out[1], out[2][None]

    in_specs = (
        P("island", "fsdp", None, None),
        P("island", None, None),
        P(None, "fsdp"),
        P(None, "fsdp"),
        P("island", None, "fsdp"),
        P("island", None, "fsdp"),
    )
    out_specs = (P(None, "fsdp"), P(None, "fsdp"), P("island", None, None))
    return jax.shard_map(
        on_device, mesh=mesh, in_specs=in_specs, out_specs=out_specs, check_vma=False
    )
```

```python
import functools

import jax
import jax.numpy as jnp
from jax import lax
from jax.experimental import pallas as pl
from jax.experimental.pallas import tpu as pltpu
from jax.sharding import PartitionSpec as P

OUTER_RATE = 0.7
MOMENTUM_COEF = 0.9
MIX_WEIGHT = 0.5

MESH = pl.DeviceIdType.MESH
CHUNK = 16
LINE = 4
UNIT = 8192.0
PAIR_LOW = 2


def remote(src, dst, send, recv, device):
    return pltpu.make_async_remote_copy(
        src_ref=src, dst_ref=dst, send_sem=send, recv_sem=recv,
        device_id=device, device_id_type=MESH,
    )


def tiles_up(width, parts):
    return 128 * (-(-(width // 128) // parts))


def shift_right(value, amount):
    return lax.shift_right_arithmetic(value, jnp.full(value.shape, amount, jnp.int32))


def pack_low(value, bits, first, L):
    low = jnp.bitwise_and(value, 2 ** bits - 1)
    width = value.shape[1]
    packed = None
    for q in range(-(-width // L)):
        piece = low[:, q * L:(q + 1) * L]
        if piece.shape[1] < L:
            piece = jnp.concatenate([piece, jnp.zeros((value.shape[0], L - piece.shape[1]), jnp.int32)], axis=1)
        piece = jnp.left_shift(piece, bits * (first + q))
        packed = piece if packed is None else packed + piece
    return packed


def unpack(high, packed, bits, first, L):
    width = high.shape[1]
    low = [jnp.bitwise_and(shift_right(packed, bits * (first + q)), 2 ** bits - 1)
           for q in range(-(-width // L))]
    low = jnp.concatenate(low, axis=1)[:, :width]
    return jnp.left_shift(high.astype(jnp.int32), bits) + low


class Part:
    NAMES = (
        "mine", "peer", "sb", "rb", "sa", "ra", "acc", "own_q", "sx", "rx", "gat",
        "l1", "s1", "r1", "s2", "r2", "s3", "r3", "s4", "r4",
        "s5", "r5", "s6", "r6", "s7", "r7", "s8", "r8",
    )

    def __init__(self, offset, width, refs):
        self.offset, self.W = offset, width
        for name, ref in zip(self.NAMES, refs):
            setattr(self, name, ref)


def part_widths(width):
    first = 256 * (-(-(width // 128) // 4))
    return [first, width - first]


def kernel(A, B, I, WW, R, grads, inner, outer_hbm, moment_hbm, draws_hbm, exps,
           new_outer, new_moment, mixed, blend, outer, moment, draws, load_sem, *refs):
    AB = A * B
    ZB = (2 * B).bit_length()
    count = len(Part.NAMES)
    parts, offset = [], 0
    for p, width in enumerate(part_widths(WW)):
        parts.append(Part(offset, width, refs[p * count:(p + 1) * count]))
        offset += width
    chunks = [(r, part) for r in range(R) for part in parts]
    isl = lax.axis_index("island")
    f = lax.axis_index("fsdp")
    h = lax.rem(isl, 2)
    c = lax.rem(f, 2)
    ab = f // 2
    b = lax.rem(ab, B)
    a = ab // B
    core_dev = (isl, 2 * ab + 1 - c)
    twin_dev = (isl + 1 - 2 * h, f)

    def b_dev(k):
        return (isl, (a * B + lax.rem(b + k, B)) * 2 + c)

    def a_dev(k):
        return (isl, (lax.rem(a + k, A) * B + b) * 2 + c)

    def i_dev(k):
        return (lax.rem(isl + k, I), f)

    partners = ([core_dev] + [b_dev(k) for k in range(1, B)] + [a_dev(k) for k in range(1, A)]
                + [i_dev(k) for k in range(1, I)])

    def rows(r):
        return pl.ds(r * CHUNK, CHUNK)

    def source(r, g, block):
        return grads.at[rows(r), pl.ds(pl.multiple_of(block * WW + g.offset, 128), g.W)]

    def start_local(r, g):
        for j in range(AB):
            pltpu.make_async_copy(source(r, g, 2 * j + c), g.mine.at[r, j], g.l1.at[r]).start()

    def start_core(r, g):
        for j in range(AB):
            remote(source(r, g, 2 * j + 1 - c), g.peer.at[r, j], g.s1.at[r], g.r1.at[r], core_dev).start()

    ahead = 2
    for q in range(ahead):
        start_local(*chunks[q])

    barrier = pltpu.get_barrier_semaphore()
    for device in partners:
        pl.semaphore_signal(barrier, inc=1, device_id=device, device_id_type=MESH)
    pl.semaphore_wait(barrier, len(partners))

    sends = []

    def begin(copy):
        copy.start()
        sends.append(copy)

    for q in range(ahead):
        start_core(*chunks[q])

    loads = [pltpu.make_async_copy(src, dst, load_sem.at[q]) for q, (src, dst) in enumerate(
        ((draws_hbm, draws), (outer_hbm, outer), (moment_hbm, moment), (inner, blend)))]

    def pair_sum(r, g, block):
        total = g.mine[r, block].astype(jnp.float32) + g.peer[r, block].astype(jnp.float32)
        return (total * UNIT).astype(jnp.int32)

    def stage1(r, g):
        pltpu.make_async_copy(g.mine.at[r], g.mine.at[r], g.l1.at[r]).wait()
        remote(g.peer.at[r], g.peer.at[r], g.s1.at[r], g.r1.at[r], core_dev).wait_recv()
        for k in range(1, B):
            target = lax.rem(b + k, B)
            low = None
            for j in range(A):
                s = pair_sum(r, g, j * B + target)
                g.sb[r, k - 1, :, j * g.W:(j + 1) * g.W] = shift_right(s, PAIR_LOW).astype(jnp.int16)
                part = pack_low(s, PAIR_LOW, 2 * j, tiles_up(g.W, 2))
                low = part if low is None else low + part
            g.sb[r, k - 1, :, A * g.W:] = low.astype(jnp.int16)
            begin(remote(g.sb.at[r, k - 1], g.rb.at[r, k - 1], g.s2.at[r, k - 1], g.r2.at[r, k - 1], b_dev(k)))

    def stage2(r, g):
        for k in range(1, B):
            remote(g.sb.at[r, k - 1], g.rb.at[r, k - 1], g.s2.at[r, k - 1], g.r2.at[r, k - 1], b_dev(k)).wait_recv()

        def column_sum(j):
            s = pair_sum(r, g, j * B + b)
            for k in range(1, B):
                s = s + unpack(g.rb[r, k - 1, :, pl.ds(pl.multiple_of(j * g.W, 128), g.W)], g.rb[r, k - 1, :, A * g.W:].astype(jnp.int32),
                               PAIR_LOW, 2 * j, tiles_up(g.W, 2))
            return s

        for k in range(1, A):
            s = column_sum(lax.rem(a + k, A))
            g.sa[r, k - 1, :, :g.W] = shift_right(s, ZB).astype(jnp.int16)
            g.sa[r, k - 1, :, g.W:] = pack_low(s, ZB, 0, tiles_up(g.W, 16 // ZB)).astype(jnp.int16)
            begin(remote(g.sa.at[r, k - 1], g.ra.at[r, k - 1], g.s3.at[r, k - 1], g.r3.at[r, k - 1], a_dev(k)))
        g.acc[r] = column_sum(a)

    def powers(r, g, sign):
        e = exps[r * CHUNK:(r + 1) * CHUNK, :]
        p = jnp.left_shift(jnp.ones_like(e), 8 + sign * e).astype(jnp.float32) / 256.0
        return jnp.concatenate(
            [jnp.broadcast_to(p[:, t:t + 1], (CHUNK, 128))
             for t in range(g.offset // 128, (g.offset + g.W) // 128)], axis=1)

    def stage3(r, g):
        if r == 0 and g.offset == 0:
            loads[0].wait()
        total = g.acc[r]
        for k in range(1, A):
            remote(g.sa.at[r, k - 1], g.ra.at[r, k - 1], g.s3.at[r, k - 1], g.r3.at[r, k - 1], a_dev(k)).wait_recv()
            total = total + unpack(g.ra[r, k - 1, :, :g.W], g.ra[r, k - 1, :, g.W:].astype(jnp.int32), ZB, 0, tiles_up(g.W, 16 // ZB))
        pseudo = total.astype(jnp.float32) * (1.0 / UNIT)
        dither = draws[r * CHUNK:(r + 1) * CHUNK, g.offset:g.offset + g.W].astype(jnp.float32) * (1.0 / 256.0)
        levels = jnp.clip(jnp.floor(pseudo * powers(r, g, -1) + dither), -127.0, 127.0)
        dequant = levels * powers(r, g, 1)
        g.own_q[r] = dequant
        g.sx[r] = dequant.astype(jnp.bfloat16)
        for k in range(1, I):
            begin(remote(g.sx.at[r], g.rx.at[r, k - 1], g.s4.at[r, k - 1], g.r4.at[r, k - 1], i_dev(k)))

    def stage4(r, g):
        if r == 0 and g.offset == 0:
            loads[1].wait()
            loads[2].wait()
        total = g.own_q[r]
        for k in range(1, I):
            remote(g.sx.at[r], g.rx.at[r, k - 1], g.s4.at[r, k - 1], g.r4.at[r, k - 1], i_dev(k)).wait_recv()
            total = total + g.rx[r, k - 1].astype(jnp.float32)
        average = total / I
        at = (slice(r * CHUNK, (r + 1) * CHUNK), slice(g.offset, g.offset + g.W))
        H = tiles_up(g.W, 2)
        moment_next = MOMENTUM_COEF * moment[at] + average
        outer_next = outer[at] - OUTER_RATE * (average + MOMENTUM_COEF * moment_next)
        new_moment[at] = moment_next
        new_outer[at] = outer_next
        g.gat[r, h, c, b, a] = jnp.where(h == 0, outer_next[:, :H], outer_next[:, g.W - H:]).astype(jnp.bfloat16)
        for k in range(1, A):
            own = g.gat.at[r, h, c, b, a]
            begin(remote(own, own, g.s5.at[r, k - 1], g.r5.at[r, k - 1], a_dev(k)))

    def to_twin(r, g, k):
        part = g.gat.at[r, h, c, lax.rem(b + B - k, B)]
        return remote(part, part, g.s7.at[r, k], g.r7.at[r, k], twin_dev)

    def to_core(r, g, other, k):
        part = g.gat.at[r, 1 - h if other else h, c, lax.rem(b + B - k, B)]
        return remote(part, part, g.s8.at[r, other, k], g.r8.at[r, other, k], core_dev)

    def stage5(r, g):
        for k in range(1, A):
            came = g.gat.at[r, h, c, b, lax.rem(a + A - k, A)]
            remote(came, came, g.s5.at[r, k - 1], g.r5.at[r, k - 1], a_dev(k)).wait_recv()
        line = g.gat.at[r, h, c, b]
        for k in range(1, B):
            begin(remote(line, line, g.s6.at[r, k - 1], g.r6.at[r, k - 1], b_dev(k)))
        begin(to_twin(r, g, 0))
        begin(to_core(r, g, 0, 0))

    def stage6(r, g):
        for k in range(1, B):
            came = g.gat.at[r, h, c, lax.rem(b + B - k, B)]
            remote(came, came, g.s6.at[r, k - 1], g.r6.at[r, k - 1], b_dev(k)).wait_recv()
            begin(to_twin(r, g, k))
            begin(to_core(r, g, 0, k))

    def mix(r, g, core):
        H = tiles_up(g.W, 2)
        at = slice(r * CHUNK, (r + 1) * CHUNK)
        for half in range(2):
            skip = half * (2 * H - g.W)
            for y in range(B):
                for z in range(A):
                    begin_at = ((z * B + y) * 2 + core) * WW + g.offset + half * H
                    span = pl.ds(pl.multiple_of(begin_at, 128), H - skip)
                    value = MIX_WEIGHT * blend[at, span].astype(jnp.float32)
                    segment = g.gat[r, half, core, y, z, :, skip:].astype(jnp.float32)
                    mixed[at, span] = (value + (1.0 - MIX_WEIGHT) * segment).astype(jnp.bfloat16)

    def stage7(r, g):
        for k in range(B):
            came = g.gat.at[r, 1 - h, c, lax.rem(b + B - k, B)]
            remote(came, came, g.s7.at[r, k], g.r7.at[r, k], twin_dev).wait_recv()
            begin(to_core(r, g, 1, k))
        if r == 0 and g.offset == 0:
            loads[3].wait()
        mix(r, g, c)

    def stage8(r, g):
        for other in range(2):
            for k in range(B):
                came = g.gat.at[r, 1 - h if other else h, 1 - c, lax.rem(b + B - k, B)]
                remote(came, came, g.s8.at[r, other, k], g.r8.at[r, other, k], core_dev).wait_recv()
        mix(r, g, 1 - c)

    stages = [stage1, stage2, stage3, stage4, stage5, stage6, stage7, stage8]
    lags = [0, 2, 4, 5, 6, 7, 8, 9]
    for t in range(len(chunks) + lags[-1]):
        for stage, lag in zip(stages, lags):
            if 0 <= t - lag < len(chunks):
                stage(*chunks[t - lag])
            if lag == 0 and t + ahead < len(chunks):
                start_local(*chunks[t + ahead])
                start_core(*chunks[t + ahead])
        if t == 1:
            for load in loads:
                load.start()

    for copy in sends:
        copy.wait_send()
    for r, g in chunks:
        remote(g.peer.at[r], g.peer.at[r], g.s1.at[r], g.r1.at[r], core_dev).wait_send()


def part_scratch(A, B, I, W, R):
    bf16, i16, f32, i32 = jnp.bfloat16, jnp.int16, jnp.float32, jnp.int32
    dma = pltpu.SemaphoreType.DMA
    bm, im = max(B - 1, 1), max(I - 1, 1)
    PL, ZL = tiles_up(W, 2), tiles_up(W, 16 // (2 * B).bit_length())
    return [
        pltpu.VMEM((R, A * B, CHUNK, W), bf16),
        pltpu.VMEM((R, A * B, CHUNK, W), bf16),
        pltpu.VMEM((R, bm, CHUNK, A * W + PL), i16),
        pltpu.VMEM((R, bm, CHUNK, A * W + PL), i16),
        pltpu.VMEM((R, A - 1, CHUNK, W + ZL), i16),
        pltpu.VMEM((R, A - 1, CHUNK, W + ZL), i16),
        pltpu.VMEM((R, CHUNK, W), i32),
        pltpu.VMEM((R, CHUNK, W), f32),
        pltpu.VMEM((R, CHUNK, W), bf16),
        pltpu.VMEM((R, im, CHUNK, W), bf16),
        pltpu.VMEM((R, 2, 2, B, A, CHUNK, PL), bf16),
        dma((R,)), dma((R,)), dma((R,)),
        dma((R, bm)), dma((R, bm)),
        dma((R, A - 1)), dma((R, A - 1)),
        dma((R, im)), dma((R, im)),
        dma((R, A - 1)), dma((R, A - 1)),
        dma((R, bm)), dma((R, bm)),
        dma((R, B)), dma((R, B)),
        dma((R, 2, B)), dma((R, 2, B)),
    ]


def solution(mesh):
    I, n = mesh.shape["island"], mesh.shape["fsdp"]
    A = LINE
    B = n // (2 * A)

    def on_device(grads, inner, outer, moment, draws, exps):
        height, W = outer.shape
        R = height // CHUNK
        any_spec = pl.BlockSpec(memory_space=pl.ANY)
        vmem = pl.BlockSpec(memory_space=pltpu.VMEM)
        bf16, i16, f32, i32 = jnp.bfloat16, jnp.int16, jnp.float32, jnp.int32
        dma = pltpu.SemaphoreType.DMA
        out = pl.pallas_call(
            functools.partial(kernel, A, B, I, W, R),
            out_shape=(
                jax.ShapeDtypeStruct(outer.shape, f32),
                jax.ShapeDtypeStruct(moment.shape, f32),
                jax.ShapeDtypeStruct(inner.shape[1:], bf16),
            ),
            in_specs=[any_spec, any_spec, any_spec, any_spec, any_spec, vmem],
            out_specs=(vmem, vmem, vmem),
            scratch_shapes=[
                pltpu.VMEM(inner.shape[1:], bf16),
                pltpu.VMEM(outer.shape, f32),
                pltpu.VMEM(outer.shape, f32),
                pltpu.VMEM(outer.shape, i32),
                dma((4,)),
            ] + [shape for width in part_widths(W) for shape in part_scratch(A, B, I, width, R)],
            compiler_params=pltpu.CompilerParams(
                collective_id=0, has_side_effects=True, vmem_limit_bytes=48 * 1024 * 1024,
            ),
        )(grads[0, 0], inner[0], outer, moment, draws[0], exps[0])
        return out[0], out[1], out[2][None]

    in_specs = (
        P("island", "fsdp", None, None),
        P("island", None, None),
        P(None, "fsdp"),
        P(None, "fsdp"),
        P("island", None, "fsdp"),
        P("island", None, "fsdp"),
    )
    out_specs = (P(None, "fsdp"), P(None, "fsdp"), P("island", None, None))
    return jax.shard_map(
        on_device, mesh=mesh, in_specs=in_specs, out_specs=out_specs, check_vma=False
    )
```

```python
import functools

import jax
import jax.numpy as jnp
from jax import lax
from jax.experimental import pallas as pl
from jax.experimental.pallas import tpu as pltpu
from jax.sharding import PartitionSpec as P

OUTER_RATE = 0.7
MOMENTUM_COEF = 0.9
MIX_WEIGHT = 0.5

MESH = pl.DeviceIdType.MESH
CHUNK = 16
LINE = 4
UNIT = 8192.0
PAIR_LOW = 2


def remote(src, dst, send, recv, device):
    return pltpu.make_async_remote_copy(
        src_ref=src, dst_ref=dst, send_sem=send, recv_sem=recv,
        device_id=device, device_id_type=MESH,
    )


def tiles_up(width, parts):
    return 128 * (-(-(width // 128) // parts))


def shift_right(value, amount):
    return lax.shift_right_arithmetic(value, jnp.full(value.shape, amount, jnp.int32))


def pack_low(value, bits, first, L):
    low = jnp.bitwise_and(value, 2 ** bits - 1)
    width = value.shape[1]
    packed = None
    for q in range(-(-width // L)):
        piece = low[:, q * L:(q + 1) * L]
        if piece.shape[1] < L:
            piece = jnp.concatenate([piece, jnp.zeros((value.shape[0], L - piece.shape[1]), jnp.int32)], axis=1)
        piece = jnp.left_shift(piece, bits * (first + q))
        packed = piece if packed is None else packed + piece
    return packed


def unpack(high, packed, bits, first, L):
    width = high.shape[1]
    low = [jnp.bitwise_and(shift_right(packed, bits * (first + q)), 2 ** bits - 1)
           for q in range(-(-width // L))]
    low = jnp.concatenate(low, axis=1)[:, :width]
    return jnp.left_shift(high.astype(jnp.int32), bits) + low


class Part:
    NAMES = (
        "mine", "peer", "sb", "rb", "sa", "ra", "acc", "own_q", "sx", "rx", "gat",
        "l1", "s1", "r1", "s2", "r2", "s3", "r3", "s4", "r4",
        "s5", "r5", "s6", "r6", "s7", "r7", "s8", "r8",
    )

    def __init__(self, offset, width, refs):
        self.offset, self.W = offset, width
        for name, ref in zip(self.NAMES, refs):
            setattr(self, name, ref)


def part_widths(width):
    first = 256 * (-(-(width // 128) // 4))
    return [first, width - first]


def kernel(A, B, I, WW, R, grads, inner, outer_hbm, moment_hbm, draws_hbm, exps,
           new_outer, new_moment, mixed, blend, outer, moment, draws, load_sem, *refs):
    AB = A * B
    ZB = (2 * B).bit_length()
    count = len(Part.NAMES)
    parts, offset = [], 0
    for p, width in enumerate(part_widths(WW)):
        parts.append(Part(offset, width, refs[p * count:(p + 1) * count]))
        offset += width
    chunks = [(r, part) for r in range(R) for part in parts]
    isl = lax.axis_index("island")
    f = lax.axis_index("fsdp")
    h = lax.rem(isl, 2)
    c = lax.rem(f, 2)
    ab = f // 2
    b = lax.rem(ab, B)
    a = ab // B
    core_dev = (isl, 2 * ab + 1 - c)
    twin_dev = (isl + 1 - 2 * h, f)

    def b_dev(k):
        return (isl, (a * B + lax.rem(b + k, B)) * 2 + c)

    def a_dev(k):
        return (isl, (lax.rem(a + k, A) * B + b) * 2 + c)

    def i_dev(k):
        return (lax.rem(isl + k, I), f)

    partners = ([core_dev] + [b_dev(k) for k in range(1, B)] + [a_dev(k) for k in range(1, A)]
                + [i_dev(k) for k in range(1, I)])

    def rows(r):
        return pl.ds(r * CHUNK, CHUNK)

    def source(r, g, block):
        return grads.at[rows(r), pl.ds(pl.multiple_of(block * WW + g.offset, 128), g.W)]

    def start_local(r, g):
        for j in range(AB):
            pltpu.make_async_copy(source(r, g, 2 * j + c), g.mine.at[r, j], g.l1.at[r]).start()

    def start_core(r, g):
        for j in range(AB):
            remote(source(r, g, 2 * j + 1 - c), g.peer.at[r, j], g.s1.at[r], g.r1.at[r], core_dev).start()

    ahead = 2
    for q in range(ahead):
        start_local(*chunks[q])

    barrier = pltpu.get_barrier_semaphore()
    for device in partners:
        pl.semaphore_signal(barrier, inc=1, device_id=device, device_id_type=MESH)
    pl.semaphore_wait(barrier, len(partners))

    sends = []

    def begin(copy):
        copy.start()
        sends.append(copy)

    for q in range(ahead):
        start_core(*chunks[q])

    loads = [pltpu.make_async_copy(src, dst, load_sem.at[q]) for q, (src, dst) in enumerate(
        ((draws_hbm, draws), (outer_hbm, outer), (moment_hbm, moment), (inner, blend)))]

    def pair_sum(r, g, block):
        total = g.mine[r, block].astype(jnp.float32) + g.peer[r, block].astype(jnp.float32)
        return (total * UNIT).astype(jnp.int32)

    def stage1(r, g):
        pltpu.make_async_copy(g.mine.at[r], g.mine.at[r], g.l1.at[r]).wait()
        remote(g.peer.at[r], g.peer.at[r], g.s1.at[r], g.r1.at[r], core_dev).wait_recv()
        for k in range(1, B):
            target = lax.rem(b + k, B)
            low = None
            for j in range(A):
                s = pair_sum(r, g, j * B + target)
                g.sb[r, k - 1, :, j * g.W:(j + 1) * g.W] = shift_right(s, PAIR_LOW).astype(jnp.int16)
                part = pack_low(s, PAIR_LOW, 2 * j, tiles_up(g.W, 2))
                low = part if low is None else low + part
            g.sb[r, k - 1, :, A * g.W:] = low.astype(jnp.int16)
            begin(remote(g.sb.at[r, k - 1], g.rb.at[r, k - 1], g.s2.at[r, k - 1], g.r2.at[r, k - 1], b_dev(k)))

    def stage2(r, g):
        for k in range(1, B):
            remote(g.sb.at[r, k - 1], g.rb.at[r, k - 1], g.s2.at[r, k - 1], g.r2.at[r, k - 1], b_dev(k)).wait_recv()

        def column_sum(j):
            s = pair_sum(r, g, j * B + b)
            for k in range(1, B):
                s = s + unpack(g.rb[r, k - 1, :, pl.ds(pl.multiple_of(j * g.W, 128), g.W)], g.rb[r, k - 1, :, A * g.W:].astype(jnp.int32),
                               PAIR_LOW, 2 * j, tiles_up(g.W, 2))
            return s

        for k in range(1, A):
            s = column_sum(lax.rem(a + k, A))
            g.sa[r, k - 1, :, :g.W] = shift_right(s, ZB).astype(jnp.int16)
            g.sa[r, k - 1, :, g.W:] = pack_low(s, ZB, 0, tiles_up(g.W, 16 // ZB)).astype(jnp.int16)
            begin(remote(g.sa.at[r, k - 1], g.ra.at[r, k - 1], g.s3.at[r, k - 1], g.r3.at[r, k - 1], a_dev(k)))
        g.acc[r] = column_sum(a)

    def powers(r, g, sign):
        e = exps[r * CHUNK:(r + 1) * CHUNK, :]
        p = jnp.left_shift(jnp.ones_like(e), 8 + sign * e).astype(jnp.float32) / 256.0
        return jnp.concatenate(
            [jnp.broadcast_to(p[:, t:t + 1], (CHUNK, 128))
             for t in range(g.offset // 128, (g.offset + g.W) // 128)], axis=1)

    def stage3(r, g):
        if r == 0 and g.offset == 0:
            loads[0].wait()
        total = g.acc[r]
        for k in range(1, A):
            remote(g.sa.at[r, k - 1], g.ra.at[r, k - 1], g.s3.at[r, k - 1], g.r3.at[r, k - 1], a_dev(k)).wait_recv()
            total = total + unpack(g.ra[r, k - 1, :, :g.W], g.ra[r, k - 1, :, g.W:].astype(jnp.int32), ZB, 0, tiles_up(g.W, 16 // ZB))
        pseudo = total.astype(jnp.float32) * (1.0 / UNIT)
        dither = draws[r * CHUNK:(r + 1) * CHUNK, g.offset:g.offset + g.W].astype(jnp.float32) * (1.0 / 256.0)
        levels = jnp.clip(jnp.floor(pseudo * powers(r, g, -1) + dither), -127.0, 127.0)
        dequant = levels * powers(r, g, 1)
        g.own_q[r] = dequant
        g.sx[r] = dequant.astype(jnp.bfloat16)
        for k in range(1, I):
            begin(remote(g.sx.at[r], g.rx.at[r, k - 1], g.s4.at[r, k - 1], g.r4.at[r, k - 1], i_dev(k)))

    def stage4(r, g):
        if r == 0 and g.offset == 0:
            loads[1].wait()
            loads[2].wait()
        total = g.own_q[r]
        for k in range(1, I):
            remote(g.sx.at[r], g.rx.at[r, k - 1], g.s4.at[r, k - 1], g.r4.at[r, k - 1], i_dev(k)).wait_recv()
            total = total + g.rx[r, k - 1].astype(jnp.float32)
        average = total / I
        at = (slice(r * CHUNK, (r + 1) * CHUNK), slice(g.offset, g.offset + g.W))
        H = tiles_up(g.W, 2)
        moment_next = MOMENTUM_COEF * moment[at] + average
        outer_next = outer[at] - OUTER_RATE * (average + MOMENTUM_COEF * moment_next)
        new_moment[at] = moment_next
        new_outer[at] = outer_next
        g.gat[r, h, c, b, a] = jnp.where(h == 0, outer_next[:, :H], outer_next[:, g.W - H:]).astype(jnp.bfloat16)
        for k in range(1, A):
            own = g.gat.at[r, h, c, b, a]
            begin(remote(own, own, g.s5.at[r, k - 1], g.r5.at[r, k - 1], a_dev(k)))

    def to_twin(r, g, k):
        part = g.gat.at[r, h, c, lax.rem(b + B - k, B)]
        return remote(part, part, g.s7.at[r, k], g.r7.at[r, k], twin_dev)

    def to_core(r, g, other, k):
        part = g.gat.at[r, 1 - h if other else h, c, lax.rem(b + B - k, B)]
        return remote(part, part, g.s8.at[r, other, k], g.r8.at[r, other, k], core_dev)

    def stage5(r, g):
        for k in range(1, A):
            came = g.gat.at[r, h, c, b, lax.rem(a + A - k, A)]
            remote(came, came, g.s5.at[r, k - 1], g.r5.at[r, k - 1], a_dev(k)).wait_recv()
        line = g.gat.at[r, h, c, b]
        for k in range(1, B):
            begin(remote(line, line, g.s6.at[r, k - 1], g.r6.at[r, k - 1], b_dev(k)))
        begin(to_twin(r, g, 0))
        begin(to_core(r, g, 0, 0))

    def stage6(r, g):
        for k in range(1, B):
            came = g.gat.at[r, h, c, lax.rem(b + B - k, B)]
            remote(came, came, g.s6.at[r, k - 1], g.r6.at[r, k - 1], b_dev(k)).wait_recv()
            begin(to_twin(r, g, k))
            begin(to_core(r, g, 0, k))

    def mix(r, g, core):
        H = tiles_up(g.W, 2)
        at = slice(r * CHUNK, (r + 1) * CHUNK)
        for half in range(2):
            skip = half * (2 * H - g.W)
            for y in range(B):
                for z in range(A):
                    begin_at = ((z * B + y) * 2 + core) * WW + g.offset + half * H
                    span = pl.ds(pl.multiple_of(begin_at, 128), H - skip)
                    value = MIX_WEIGHT * blend[at, span].astype(jnp.float32)
                    segment = g.gat[r, half, core, y, z, :, skip:].astype(jnp.float32)
                    mixed[at, span] = (value + (1.0 - MIX_WEIGHT) * segment).astype(jnp.bfloat16)

    def stage7(r, g):
        for k in range(B):
            came = g.gat.at[r, 1 - h, c, lax.rem(b + B - k, B)]
            remote(came, came, g.s7.at[r, k], g.r7.at[r, k], twin_dev).wait_recv()
            begin(to_core(r, g, 1, k))
        if r == 0 and g.offset == 0:
            loads[3].wait()
        mix(r, g, c)

    def stage8(r, g):
        for other in range(2):
            for k in range(B):
                came = g.gat.at[r, 1 - h if other else h, 1 - c, lax.rem(b + B - k, B)]
                remote(came, came, g.s8.at[r, other, k], g.r8.at[r, other, k], core_dev).wait_recv()
        mix(r, g, 1 - c)

    stages = [stage1, stage2, stage3, stage4, stage5, stage6, stage7, stage8]
    lags = [0, 1, 2, 3, 4, 5, 6, 7]
    for t in range(len(chunks) + lags[-1]):
        for stage, lag in zip(stages, lags):
            if 0 <= t - lag < len(chunks):
                stage(*chunks[t - lag])
            if lag == 0 and t + ahead < len(chunks):
                start_local(*chunks[t + ahead])
                start_core(*chunks[t + ahead])
        if t == 1:
            for load in loads:
                load.start()

    for copy in sends:
        copy.wait_send()
    for r, g in chunks:
        remote(g.peer.at[r], g.peer.at[r], g.s1.at[r], g.r1.at[r], core_dev).wait_send()


def part_scratch(A, B, I, W, R):
    bf16, i16, f32, i32 = jnp.bfloat16, jnp.int16, jnp.float32, jnp.int32
    dma = pltpu.SemaphoreType.DMA
    bm, im = max(B - 1, 1), max(I - 1, 1)
    PL, ZL = tiles_up(W, 2), tiles_up(W, 16 // (2 * B).bit_length())
    return [
        pltpu.VMEM((R, A * B, CHUNK, W), bf16),
        pltpu.VMEM((R, A * B, CHUNK, W), bf16),
        pltpu.VMEM((R, bm, CHUNK, A * W + PL), i16),
        pltpu.VMEM((R, bm, CHUNK, A * W + PL), i16),
        pltpu.VMEM((R, A - 1, CHUNK, W + ZL), i16),
        pltpu.VMEM((R, A - 1, CHUNK, W + ZL), i16),
        pltpu.VMEM((R, CHUNK, W), i32),
        pltpu.VMEM((R, CHUNK, W), f32),
        pltpu.VMEM((R, CHUNK, W), bf16),
        pltpu.VMEM((R, im, CHUNK, W), bf16),
        pltpu.VMEM((R, 2, 2, B, A, CHUNK, PL), bf16),
        dma((R,)), dma((R,)), dma((R,)),
        dma((R, bm)), dma((R, bm)),
        dma((R, A - 1)), dma((R, A - 1)),
        dma((R, im)), dma((R, im)),
        dma((R, A - 1)), dma((R, A - 1)),
        dma((R, bm)), dma((R, bm)),
        dma((R, B)), dma((R, B)),
        dma((R, 2, B)), dma((R, 2, B)),
    ]


def solution(mesh):
    I, n = mesh.shape["island"], mesh.shape["fsdp"]
    A = LINE
    B = n // (2 * A)

    def on_device(grads, inner, outer, moment, draws, exps):
        height, W = outer.shape
        R = height // CHUNK
        any_spec = pl.BlockSpec(memory_space=pl.ANY)
        vmem = pl.BlockSpec(memory_space=pltpu.VMEM)
        bf16, i16, f32, i32 = jnp.bfloat16, jnp.int16, jnp.float32, jnp.int32
        dma = pltpu.SemaphoreType.DMA
        out = pl.pallas_call(
            functools.partial(kernel, A, B, I, W, R),
            out_shape=(
                jax.ShapeDtypeStruct(outer.shape, f32),
                jax.ShapeDtypeStruct(moment.shape, f32),
                jax.ShapeDtypeStruct(inner.shape[1:], bf16),
            ),
            in_specs=[any_spec, any_spec, any_spec, any_spec, any_spec, vmem],
            out_specs=(vmem, vmem, vmem),
            scratch_shapes=[
                pltpu.VMEM(inner.shape[1:], bf16),
                pltpu.VMEM(outer.shape, f32),
                pltpu.VMEM(outer.shape, f32),
                pltpu.VMEM(outer.shape, i32),
                dma((4,)),
            ] + [shape for width in part_widths(W) for shape in part_scratch(A, B, I, width, R)],
            compiler_params=pltpu.CompilerParams(
                collective_id=0, has_side_effects=True, vmem_limit_bytes=48 * 1024 * 1024,
            ),
        )(grads[0, 0], inner[0], outer, moment, draws[0], exps[0])
        return out[0], out[1], out[2][None]

    in_specs = (
        P("island", "fsdp", None, None),
        P("island", None, None),
        P(None, "fsdp"),
        P(None, "fsdp"),
        P("island", None, "fsdp"),
        P("island", None, "fsdp"),
    )
    out_specs = (P(None, "fsdp"), P(None, "fsdp"), P("island", None, None))
    return jax.shard_map(
        on_device, mesh=mesh, in_specs=in_specs, out_specs=out_specs, check_vma=False
    )
```
